768 devices in a mesh: gx: 96 (over y, z), gy: 8 (over x, core).
Axes of the slice: x: 4, y: 8, z: 12, core: 2. Of those that a mesh axis runs over, the one named last changes fastest.
Arguments:
- disp: bfloat16 [49152, 4096], P(('gx', 'gy')), may hold values from -6 to 6
- adjoint: bfloat16 [49152, 4096], P(('gx', 'gy')), may hold values from -6 to 6
- tiles: bfloat16 [73728, 4096], P(('gx', 'gy')), may hold values from -0.75 to 0.75
- tile_rows: int32 [73728], P(('gx', 'gy')), may hold values from 0 to 63
- tile_cols: int32 [73728], P(('gx', 'gy')), may hold values from 0 to 95
- density: float32 [73728], P(('gx', 'gy')), may hold values from 0.1 to 1
- filter_weight: float32 [73728], P(('gx', 'gy')), may hold values from 0.2 to 2
- owner: int32 [73728, 1], P(('gx', 'gy')), may hold values from 0 to 7; in each aligned block of 96 rows (0 to 95, 96 to 191, ...) at most 96 rows name the same one
- region: int32 [73728], P(('gx', 'gy')), may hold values from 0 to 31
- face_x: int32 [768, 2, 12], P(('gx', 'gy')), may hold values from 0 to 63
- face_y: int32 [768, 2, 4], P(('gx', 'gy')), may hold values from 0 to 63
Outputs:
- filtered: float32 [24576, 128], P(('gx', 'gy'))
- compliance: float32 [64], replicated
The draws below stay inside these ranges and needn't reach their ends.
Inputs may be any that keep to these rules, and one draw needn't show every extreme that they name: Among the 96 elements of one subdomain at most 96 name the same owner, a bound that some block reaches.
All inputs are finite; a program needn't handle non-finite values.
Results may differ from the reference program's by a relative error of at most 0.0005.
Values may be sent and summed in bfloat16 or wider, within the bound.
No kernel may reach another device: no remote copies, remote signals or barrier semaphores. Data moves between devices by JAX's collectives and lax.ppermute only.
A program may use at most 64 MiB of HBM per device.

```python
import math
import jax
import jax.numpy as jnp
import numpy as np
from jax import lax

BS = 64
R = 64
NB = 64
NT = 96
NIX = 12
NIY = 4
NREG = 32
CAP = 96
NGHOST = 96
BLOCKS = 49152
TILES = 73728
N_GX = 96
N_GY = 8
DEVICES = 768


def touch_ends(values, key, smallest, top_value):
    longest = values.shape.index(max(values.shape))
    spots = []
    for shift in (0, 1):
        where = [jax.random.randint(jax.random.fold_in(key, axis), (), 0, length) for axis, length in enumerate(values.shape)]
        where[longest] = (where[longest] + shift) % values.shape[longest]
        spots.append(tuple(where))
    return values.at[spots[0]].set(smallest).at[spots[1]].set(top_value)


def levels(stream_key, dims, pieces, least, largest):
    gain = 1.0
    for position, parts in pieces:
        steps = jax.random.uniform(jax.random.fold_in(jax.random.fold_in(stream_key, 6), position), (parts,), jnp.float32, least / len(pieces), largest / len(pieces))
        gain = gain * jnp.repeat(jnp.exp(steps), dims[position] // parts).reshape((-1,) + (1,) * (len(dims) - 1 - position))
    return gain


def deal_out(stream_key, own, number, rows, count, top, limit, lean):
    ranking = jax.random.permutation(stream_key, count)
    packed, ordinary = portions_of(count, rows * top, limit, lean, True), portions_of(count, rows * top, limit, lean, False)
    places = jnp.arange(count)

    def named(tallies, turn):
        used = int((tallies > 0).sum())
        fixed = max(1, used // 4)
        moved = fixed + (places - fixed + turn * (used - fixed)) % max(1, count - fixed)
        return jnp.zeros((count,), jnp.int32).at[ranking[jnp.where(places < fixed, places, moved)]].set(jnp.asarray(tallies, jnp.int32))

    tallies = jnp.where(number % 4 == 0, named(packed, number // 4), named(ordinary, number - number // 4 - 1))
    mixed = jax.random.permutation(jax.random.fold_in(own, 3), count)
    source_of, sink = mixed[0:count // 2 * 2:2], mixed[1:count // 2 * 2:2]
    margin = jnp.minimum(tallies[source_of] - 1, limit - tallies[sink]) // 2
    margin = jnp.where((source_of == ranking[0]) | (sink == ranking[0]) | (tallies[sink] == 0), 0, jnp.maximum(margin, 0))
    moved = jax.random.randint(jax.random.fold_in(own, 4), (count // 2,), 0, 1 << 20) % (margin + 1)
    tallies = tallies.at[source_of].add(-moved).at[sink].add(moved)
    labels = jnp.searchsorted(jnp.cumsum(tallies), jnp.arange(rows * top), side="right").astype(jnp.int32)
    table = labels.reshape(top, rows).T
    table = table[jax.random.permutation(jax.random.fold_in(own, 1), rows)]
    turn = jax.random.randint(jax.random.fold_in(own, 2), (rows, 1), 0, top)
    return jnp.take_along_axis(table, (jnp.arange(top)[None, :] + turn) % top, axis=1)


def portions_of(amount, total, most, slope, full):
    weights = [(1 << 20) // math.isqrt(grade ** slope) + 1 for grade in range(1, amount + 1)]
    largest = most if full else min(most, max(-(-total // amount), total * weights[0] // sum(weights)))
    least = 1 if total - largest >= amount - 1 else 0
    holding, surplus = [largest] + [least] * (amount - 1), total - largest - least * (amount - 1)
    while surplus > 0:
        free = [i for i in range(1, amount) if holding[i] < largest] or [i for i in range(1, amount) if holding[i] < most]
        whole, remaining = sum([weights[i] for i in free]), surplus
        for i in free:
            extra = min(most - holding[i], max(1, remaining * weights[i] // whole), surplus)
            holding[i] = holding[i] + extra
            surplus = surplus - extra
    return np.array(holding)


def centred(key, dims, spread, bound, pieces=(), kind=jnp.bfloat16):
    loudness = levels(key, dims, pieces, -0.22, 0.18) if pieces else 1.0
    values = jax.random.normal(key, dims, jnp.float32) * spread * loudness
    return jnp.minimum(jnp.maximum(values, -bound), bound).astype(kind)


def setup_inputs(seed: int = 0) -> dict:
    streams_of = jax.random.split(jax.random.key(seed), 12)
    disp = centred(streams_of[0], (BLOCKS, BS * R), 1.0, 6.0, ((0, 768),))
    adjoint = centred(streams_of[1], (BLOCKS, BS * R), 1.0, 6.0, ((0, 768),))
    tiles = centred(streams_of[2], (TILES, BS * BS), BS ** -0.5, 0.75, ((0, 768),))
    tile_rows = touch_ends(jax.random.randint(streams_of[3], (TILES,), 0, NB), jax.random.fold_in(streams_of[3], 1), 0, NB - 1).astype(jnp.int32)
    tile_cols = touch_ends(jax.random.randint(streams_of[4], (TILES,), 0, NGHOST), jax.random.fold_in(streams_of[4], 1), 0, NGHOST - 1).astype(jnp.int32)
    density = jnp.clip(0.1 + 0.9 * jax.random.uniform(streams_of[5], (TILES,), jnp.float32) ** levels(streams_of[5], (TILES,), ((0, 768),), -0.2, 0.2), 0.1, 1.0)
    filter_weight = jnp.clip(jnp.exp(math.log(2.0) - 2.3025851 * jax.random.uniform(streams_of[6], (TILES,), jnp.float32) ** levels(streams_of[6], (TILES,), ((0, 768),), -0.2, 0.2)), 0.2, 2.0)
    owner_keys = jax.random.split(jax.random.fold_in(streams_of[7], 1), TILES // NT)
    owner_turns = jax.random.permutation(jax.random.fold_in(streams_of[7], 3), TILES // NT)
    owner = jax.vmap(lambda own, number: deal_out(jax.random.fold_in(streams_of[7], 2), own, number, NT, N_GY, 1, CAP, 2))(owner_keys, owner_turns).reshape((TILES, 1))
    region = touch_ends(jax.random.randint(streams_of[8], (TILES,), 0, NREG), jax.random.fold_in(streams_of[8], 1), 0, NREG - 1).astype(jnp.int32)
    face_x = touch_ends(jax.random.randint(streams_of[9], (DEVICES, 2, NIX), 0, NB), jax.random.fold_in(streams_of[9], 1), 0, NB - 1).astype(jnp.int32)
    face_y = touch_ends(jax.random.randint(streams_of[10], (DEVICES, 2, NIY), 0, NB), jax.random.fold_in(streams_of[10], 1), 0, NB - 1).astype(jnp.int32)
    return dict(disp=disp, adjoint=adjoint, tiles=tiles, tile_rows=tile_rows, tile_cols=tile_cols, density=density, filter_weight=filter_weight, owner=owner, region=region, face_x=face_x, face_y=face_y)


def element_terms(args):
    uext, lext, tile, rows, cols, rho, weight = args
    kmat = tile.reshape(-1, BS, BS).astype(jnp.float32)
    ucol = uext[cols].reshape(-1, BS, R).astype(jnp.float32)
    lcol = lext[cols].reshape(-1, BS, R).astype(jnp.float32)
    ku = jnp.einsum('tjk,tkr->tjr', kmat, ucol)
    kl = jnp.einsum('tjk,tkr->tjr', kmat, lcol)
    urow = uext[rows].reshape(-1, BS, R).astype(jnp.float32)
    lrow = lext[rows].reshape(-1, BS, R).astype(jnp.float32)
    cross = lax.optimization_barrier(jnp.sum(lrow * ku + urow * kl, axis=1))
    energy = lax.optimization_barrier(jnp.sum(urow * ku, axis=1)) / math.sqrt(BS)
    sens = -(3.0 * rho * rho / (2.0 * math.sqrt(BS)))[:, None] * cross
    payload = weight[:, None] * jnp.concatenate([sens, energy], axis=1)
    return (payload, lax.optimization_barrier(jnp.sum(energy, axis=0)))

def extend(blocks, face_x, face_y):
    pick = jax.vmap(jax.vmap(lambda source, index: source[index]))
    sent_up_x = pick(blocks, face_x[:, :, 0])
    sent_down_x = pick(blocks, face_x[:, :, 1])
    sent_up_y = pick(blocks, face_y[:, :, 0])
    sent_down_y = pick(blocks, face_y[:, :, 1])
    low_x = jnp.concatenate([jnp.zeros_like(sent_up_x[:1]), sent_up_x[:-1]], axis=0)
    high_x = jnp.concatenate([sent_down_x[1:], jnp.zeros_like(sent_down_x[:1])], axis=0)
    low_y = jnp.concatenate([jnp.zeros_like(sent_up_y[:, :1]), sent_up_y[:, :-1]], axis=1)
    high_y = jnp.concatenate([sent_down_y[:, 1:], jnp.zeros_like(sent_down_y[:, :1])], axis=1)
    return jnp.concatenate([blocks, low_x, high_x, low_y, high_y], axis=2)

def reference(disp, adjoint, tiles, tile_rows, tile_cols, density, filter_weight, owner, region, face_x, face_y):
    count_x = N_GX
    count_y = N_GY
    ndev = count_x * count_y
    fx = face_x.reshape(count_x, count_y, 2, NIX)
    fy = face_y.reshape(count_x, count_y, 2, NIY)
    uext = extend(disp.reshape(count_x, count_y, NB, BS * R), fx, fy).reshape(ndev, NGHOST, BS * R)
    lext = extend(adjoint.reshape(count_x, count_y, NB, BS * R), fx, fy).reshape(ndev, NGHOST, BS * R)
    payload, energy = lax.map(element_terms, (uext, lext, tiles.reshape(ndev, NT, BS * BS), tile_rows.reshape(ndev, NT), tile_cols.reshape(ndev, NT), density.reshape(ndev, NT), filter_weight.reshape(ndev, NT)))
    column_base = jnp.arange(ndev, dtype=jnp.int32) // count_y * count_y
    owner_dev = column_base[:, None] + owner.reshape(ndev, NT)
    global_id = (owner_dev * NREG + region.reshape(ndev, NT)).reshape(-1)
    sums = jax.ops.segment_sum(payload.reshape(-1, 2 * R), global_id, ndev * NREG)
    totals = jax.ops.segment_sum(filter_weight, global_id, ndev * NREG)
    filtered = sums / jnp.maximum(totals, 1.0)[:, None]
    compliance = lax.optimization_barrier(jnp.sum(energy, axis=0)) / math.sqrt(ndev * NT)
    return (filtered, compliance)
```

```python
import math

import jax
import jax.numpy as jnp
from jax import lax
from jax.experimental import pallas as pl
from jax.experimental.pallas import tpu as pltpu
from jax.sharding import PartitionSpec as P

BS = 64
R = 64
NREG = 32
NB = 64
NT = 96
LANES = 128
F32 = jnp.float32
BF16 = jnp.bfloat16
ROWS = 40


def left_half(shape):
    return lax.broadcasted_iota(jnp.int32, shape, 1) < R


def pack_kernel(fx_ref, fy_ref, disp_ref, adj_ref, ul_ref, xu_ref, xd_ref, yu_ref, yd_ref, scr):
    left = left_half((NB, LANES))
    for c in range(BS // 2):
        cols = slice(LANES * c, LANES * (c + 1))
        u = disp_ref[:, cols].astype(F32)
        v = adj_ref[:, cols].astype(F32)
        scr[pl.ds(2 * c, NB, stride=BS), :] = jnp.where(left, u, pltpu.roll(v, R, 1))
        scr[pl.ds(2 * c + 1, NB, stride=BS), :] = jnp.where(left, pltpu.roll(u, R, 1), v)
    ul_ref[...] = scr[...].astype(BF16)
    for out, idx, side, n in ((xu_ref, fx_ref, 0, 12), (xd_ref, fx_ref, 1, 12), (yu_ref, fy_ref, 0, 4), (yd_ref, fy_ref, 1, 4)):
        for i in range(n):
            out[i * BS:(i + 1) * BS, :] = ul_ref[pl.ds(pl.multiple_of(idx[0, side, i] * BS, BS), BS), :]


def pack(face_x, face_y, disp, adjoint):
    smem = pl.BlockSpec(memory_space=pltpu.SMEM)
    vmem = pl.BlockSpec(memory_space=pltpu.VMEM)
    sizes = (NB, 12, 12, 4, 4)
    return pl.pallas_call(
        pack_kernel,
        out_shape=[jax.ShapeDtypeStruct((n * BS, LANES), BF16) for n in sizes],
        in_specs=[smem, smem, vmem, vmem],
        out_specs=[vmem] * 5,
        scratch_shapes=[pltpu.VMEM((NB * BS, LANES), F32)],
        compiler_params=pltpu.CompilerParams(vmem_limit_bytes=16 << 20),
    )(face_x, face_y, disp, adjoint)


def stiffness_kernel(tiles_ref, k_ref, scr):
    for c in range(BS // 2):
        k = tiles_ref[:, LANES * c:LANES * (c + 1)].astype(F32)
        scr[pl.ds(2 * c, NT, stride=BS), :] = k
        scr[pl.ds(2 * c + 1, NT, stride=BS), :] = pltpu.roll(k, R, 1)
    k_ref[...] = scr[...].astype(BF16)


def stiffness(tiles):
    vmem = pl.BlockSpec(memory_space=pltpu.VMEM)
    return pl.pallas_call(
        stiffness_kernel,
        out_shape=jax.ShapeDtypeStruct((NT * BS, LANES), BF16),
        in_specs=[vmem],
        out_specs=vmem,
        scratch_shapes=[pltpu.VMEM((NT * BS, LANES), F32)],
        compiler_params=pltpu.CompilerParams(vmem_limit_bytes=16 << 20),
        cost_estimate=pl.CostEstimate(flops=0, bytes_accessed=8 << 20, transcendentals=0),
    )(tiles)


def column(row):
    wide = jnp.broadcast_to(row, (LANES, NT)).T
    return wide


def element_kernel(rows_ref, cols_ref, density_ref, weight_ref, owner_ref, region_ref,
                   k_ref, ul_ref, lx_ref, hx_ref, ly_ref, hy_ref, out_ref, ext, en8, cr8):
    n = NB * BS
    ext[:n, :] = ul_ref[...]
    ext[n:n + 768, :] = lx_ref[...]
    ext[n + 768:n + 1536, :] = hx_ref[...]
    ext[n + 1536:n + 1792, :] = ly_ref[...]
    ext[n + 1792:, :] = hy_ref[...]

    group = 8

    def body(g, carry):
        for i in range(group):
            t = g * group + i
            kmat = k_ref[pl.ds(pl.multiple_of(t * BS, BS), BS), :][:, :BS]
            col = ext[pl.ds(pl.multiple_of(cols_ref[t] * BS, BS), BS), :]
            row = ul_ref[pl.ds(pl.multiple_of(rows_ref[t] * BS, BS), BS), :].astype(F32)
            prod = jnp.dot(kmat, col, preferred_element_type=F32)
            same = row * prod
            other = pltpu.roll(row, R, 1) * prod
            at = pl.ds(pl.multiple_of(t * 8, 8), 8)
            en8[at, :] = jnp.sum(same.reshape(8, 8, LANES), axis=0)
            cr8[at, :] = jnp.sum(other.reshape(8, 8, LANES), axis=0)
        return carry

    lax.fori_loop(0, NT // group, body, 0)
    en = en8[pl.ds(0, NT, stride=8), :]
    cr = cr8[pl.ds(0, NT, stride=8), :]
    for s in range(1, 8):
        en = en + en8[pl.ds(s, NT, stride=8), :]
        cr = cr + cr8[pl.ds(s, NT, stride=8), :]
    left = left_half((NT, LANES))
    energy = pltpu.roll(en, R, 1) / math.sqrt(BS)
    cross = cr + pltpu.roll(cr, R, 1)
    rho = column(density_ref[...])
    weight = column(weight_ref[...])
    sens = -(3.0 * rho * rho / (2.0 * math.sqrt(BS))) * cross
    payload = weight * jnp.where(left, sens, energy)
    ident = owner_ref[...] * NREG + region_ref[...]
    onehot = (lax.broadcasted_iota(jnp.int32, (8 * NREG, NT), 0) == ident).astype(F32).astype(BF16)
    high = payload.astype(BF16)
    rest = payload - high.astype(F32)
    mid = rest.astype(BF16)
    low = (rest - mid.astype(F32)).astype(BF16)
    sums = (jnp.dot(onehot, high, preferred_element_type=F32)
            + jnp.dot(onehot, mid, preferred_element_type=F32)
            + jnp.dot(onehot, low, preferred_element_type=F32))
    ident_col = column(ident.astype(F32)).astype(jnp.int32)
    lane = lax.broadcasted_iota(jnp.int32, (NT, LANES), 1)
    total_energy = jnp.sum(energy, axis=0, keepdims=True)
    sub = lax.broadcasted_iota(jnp.int32, (8, LANES), 0)
    for o in range(8):
        out_ref[o, :NREG, :] = sums[o * NREG:(o + 1) * NREG, :]
        hit = (ident_col == lane + o * NREG) & (lane < NREG)
        totals = jnp.sum(jnp.where(hit, weight, 0.0), axis=0, keepdims=True)
        out_ref[o, NREG:, :] = jnp.where(sub == 0, totals, jnp.where(sub == 1, total_energy, 0.0))


def elements(rows, cols, density, weight, owner, region, k, ul, lx, hx, ly, hy):
    smem = pl.BlockSpec(memory_space=pltpu.SMEM)
    vmem = pl.BlockSpec(memory_space=pltpu.VMEM)
    return pl.pallas_call(
        element_kernel,
        out_shape=jax.ShapeDtypeStruct((8, ROWS, LANES), F32),
        in_specs=[smem, smem] + [vmem] * 10,
        out_specs=vmem,
        scratch_shapes=[pltpu.VMEM((96 * BS, LANES), BF16), pltpu.VMEM((NT * 8, LANES), F32), pltpu.VMEM((NT * 8, LANES), F32)],
        compiler_params=pltpu.CompilerParams(vmem_limit_bytes=16 << 20),
    )(rows, cols, density.reshape(1, NT), weight.reshape(1, NT), owner.reshape(1, NT), region.reshape(1, NT),
      k, ul, lx, hx, ly, hy)


def region_kernel(got_ref, out_ref, energy_ref):
    total = got_ref[0]
    for s in range(1, 8):
        total = total + got_ref[s]
    weights = total[NREG:NREG + 1, :NREG]
    eye = lax.broadcasted_iota(jnp.int32, (NREG, NREG), 0) == lax.broadcasted_iota(jnp.int32, (NREG, NREG), 1)
    divisor = jnp.sum(jnp.where(eye, weights, 0.0), axis=1, keepdims=True)
    out_ref[...] = total[:NREG, :] / jnp.maximum(divisor, 1.0)
    energy_ref[...] = jnp.broadcast_to(total[NREG + 1:NREG + 2, :], energy_ref.shape[:1] + (LANES,)).reshape(energy_ref.shape)


def regions(got, columns):
    vmem = pl.BlockSpec(memory_space=pltpu.VMEM)
    return pl.pallas_call(
        region_kernel,
        out_shape=[jax.ShapeDtypeStruct((NREG, LANES), F32), jax.ShapeDtypeStruct((columns, 1, LANES), F32)],
        in_specs=[vmem],
        out_specs=[vmem, vmem],
        compiler_params=pltpu.CompilerParams(vmem_limit_bytes=16 << 20),
    )(got)


def shifted(x, axis, by):
    size = lax.axis_size(axis)
    pairs = [(i, i + by) for i in range(size) if 0 <= i + by < size]
    return lax.ppermute(x, axis, pairs)


def shards(disp, adjoint, tiles, tile_rows, tile_cols, density, filter_weight, owner, region, face_x, face_y):
    ul, xu, xd, yu, yd = pack(face_x, face_y, disp, adjoint)
    low_x = shifted(xu, "gx", 1)
    high_x = shifted(xd, "gx", -1)
    low_y = shifted(yu, "gy", 1)
    high_y = shifted(yd, "gy", -1)
    k = stiffness(tiles)
    sent = elements(tile_rows, tile_cols, density, filter_weight, owner, region, k, ul, low_x, high_x, low_y, high_y)
    got = lax.all_to_all(sent, "gy", split_axis=0, concat_axis=0, tiled=True)
    columns = lax.axis_size("gx")
    filtered, energy = regions(got, columns)
    energies = lax.all_to_all(energy, "gx", split_axis=0, concat_axis=0, tiled=True)
    total_tiles = NT * columns * lax.axis_size("gy")
    compliance = jnp.sum(energies, axis=(0, 1))[R:] / math.sqrt(total_tiles)
    return (filtered, compliance)


def solution(mesh):
    flat = P(("gx", "gy"))
    wide = P(("gx", "gy"), None)
    deep = P(("gx", "gy"), None, None)
    placed = (wide, wide, wide, flat, flat, flat, flat, wide, flat, deep, deep)
    return jax.shard_map(shards, mesh=mesh, in_specs=placed, out_specs=(wide, P()), check_vma=False)
```

```python
import functools
import math

import jax
import jax.numpy as jnp
from jax import lax
from jax.experimental import pallas as pl
from jax.experimental.pallas import tpu as pltpu
from jax.sharding import Mesh, PartitionSpec as P

BS = 64
R = 64
NREG = 32
NB = 64
NT = 96
NIX = 12
NIY = 4
OWNERS = 8
LANES = 128
HALF = BS // 2
SENT_ROWS = 40
GROUP = 32
F32 = jnp.float32
BF16 = jnp.bfloat16
SMEM = pl.BlockSpec(memory_space=pltpu.SMEM)
VMEM = pl.BlockSpec(memory_space=pltpu.VMEM)
HBM = pl.BlockSpec(memory_space=pltpu.HBM)
PARAMS = pltpu.CompilerParams(vmem_limit_bytes=16 << 20)


def pack_kernel(fx_ref, fy_ref, disp_ref, adj_ref, ul_ref, x1_ref, x2_ref, y1_ref, y2_ref, disp, adj, fx, fy, sems):
    pairs = ((disp_ref, disp), (adj_ref, adj), (fx_ref, fx), (fy_ref, fy))
    copies = [pltpu.make_async_copy(src, dst, sems.at[i]) for i, (src, dst) in enumerate(pairs)]
    for copy in copies:
        copy.start()
    for copy in copies:
        copy.wait()
    u = disp[...].reshape(NB, HALF, LANES)
    v = adj[...].reshape(NB, HALF, LANES)
    ul_ref[:, :HALF, :] = jnp.concatenate([u[..., :R], v[..., :R]], axis=-1)
    ul_ref[:, HALF:, :] = jnp.concatenate([u[..., R:], v[..., R:]], axis=-1)
    odd_x = lax.rem(lax.axis_index("z"), 2)
    odd_y = lax.axis_index("c")
    for out, idx, side, count in ((x1_ref, fx, odd_x, NIX), (x2_ref, fx, 1 - odd_x, NIX),
                                  (y1_ref, fy, odd_y, NIY), (y2_ref, fy, 1 - odd_y, NIY)):
        for i in range(count):
            out[i] = ul_ref[idx[0, side, i]]


def pack(face_x, face_y, disp, adjoint):
    args = [pltpu.with_memory_space_constraint(a, pltpu.HBM) for a in (face_x, face_y, disp, adjoint)]
    return pl.pallas_call(
        pack_kernel,
        out_shape=[jax.ShapeDtypeStruct((n, BS, LANES), BF16) for n in (NB, NIX, NIX, NIY, NIY)],
        in_specs=[HBM] * 4,
        out_specs=[VMEM] * 5,
        scratch_shapes=[pltpu.VMEM((NB, BS * R), BF16), pltpu.VMEM((NB, BS * R), BF16),
                        pltpu.SMEM((1, 2, NIX), jnp.int32), pltpu.SMEM((1, 2, NIY), jnp.int32),
                        pltpu.SemaphoreType.DMA((4,))],
        compiler_params=PARAMS,
    )(*args)


def stiffness_kernel(tiles_ref, k_ref):
    pairs = tiles_ref[...].reshape(NT * HALF, LANES)
    source = lax.broadcasted_iota(jnp.int32, (LANES, 2 * LANES), 0)
    target = lax.broadcasted_iota(jnp.int32, (LANES, 2 * LANES), 1)
    lane = target % LANES
    wanted = (target // LANES) * BS + 2 * (lane % HALF) + lane // HALF
    order = ((source == wanted) & (lane < BS)).astype(F32).astype(BF16)
    moved = jnp.dot(pairs, order, preferred_element_type=F32).astype(BF16)
    k_ref[:, :HALF, :] = moved[:, :LANES].reshape(NT, HALF, LANES)
    k_ref[:, HALF:, :] = moved[:, LANES:].reshape(NT, HALF, LANES)


def stiffness(tiles):
    return pl.pallas_call(
        stiffness_kernel,
        out_shape=jax.ShapeDtypeStruct((NT, BS, LANES), BF16),
        in_specs=[VMEM],
        out_specs=VMEM,
        compiler_params=PARAMS,
        cost_estimate=pl.CostEstimate(flops=0, bytes_accessed=8 << 20, transcendentals=0),
    )(tiles)


def column(row):
    return jnp.broadcast_to(row, (LANES, NT)).T


def element_kernel(rows_ref, cols_ref, density_ref, weight_ref, owner_ref, region_ref, k_ref, ul_ref,
                   x1_ref, x2_ref, y1_ref, y2_ref, sent_ref, ext, same8, cross8):
    odd_x = lax.rem(lax.axis_index("z"), 2)
    odd_y = lax.axis_index("c")
    ext[:NB] = ul_ref[...]
    ext[pl.ds(NB + NIX * (1 - odd_x), NIX)] = x1_ref[...]
    ext[pl.ds(NB + NIX * odd_x, NIX)] = x2_ref[...]
    ext[pl.ds(NB + 2 * NIX + NIY * (1 - odd_y), NIY)] = y1_ref[...]
    ext[pl.ds(NB + 2 * NIX + NIY * odd_y, NIY)] = y2_ref[...]

    def body(g, carry):
        for i in range(GROUP):
            t = g * GROUP + i
            row = ul_ref[rows_ref[t]].astype(F32)
            prod = jnp.dot(k_ref[t][:, :BS], ext[cols_ref[t]], preferred_element_type=F32)
            at = pl.ds(pl.multiple_of(t * 8, 8), 8)
            same8[at, :] = jnp.sum((row * prod).reshape(8, 8, LANES), axis=0)
            cross8[at, :] = jnp.sum((pltpu.roll(row, R, 1) * prod).reshape(8, 8, LANES), axis=0)
        return carry

    lax.fori_loop(0, NT // GROUP, body, 0)
    same = same8[pl.ds(0, NT, stride=8), :]
    cross = cross8[pl.ds(0, NT, stride=8), :]
    for s in range(1, 8):
        same = same + same8[pl.ds(s, NT, stride=8), :]
        cross = cross + cross8[pl.ds(s, NT, stride=8), :]
    energy = same / math.sqrt(BS)
    cross = cross + pltpu.roll(cross, R, 1)
    energy_total = jnp.sum(energy, axis=0, keepdims=True)
    rho = column(density_ref[...])
    weight = column(weight_ref[...])
    sens = -(3.0 * rho * rho / (2.0 * math.sqrt(BS))) * cross
    left = lax.broadcasted_iota(jnp.int32, (NT, LANES), 1) < R
    payload = weight * jnp.where(left, sens, pltpu.roll(energy, R, 1))
    ident = owner_ref[...] * NREG + region_ref[...]
    onehot = (lax.broadcasted_iota(jnp.int32, (OWNERS * NREG, NT), 0) == ident).astype(F32).astype(BF16)
    high = payload.astype(BF16)
    rest = payload - high.astype(F32)
    mid = rest.astype(BF16)
    low = (rest - mid.astype(F32)).astype(BF16)
    sums = (jnp.dot(onehot, high, preferred_element_type=F32)
            + jnp.dot(onehot, mid, preferred_element_type=F32)
            + jnp.dot(onehot, low, preferred_element_type=F32))
    ident_column = column(ident.astype(F32)).astype(jnp.int32)
    lane = lax.broadcasted_iota(jnp.int32, (NT, LANES), 1)
    place = lax.broadcasted_iota(jnp.int32, (8, LANES), 0)
    for o in range(OWNERS):
        sent_ref[o, :NREG, :] = sums[o * NREG:(o + 1) * NREG, :]
        hit = (ident_column == lane + o * NREG) & (lane < NREG)
        totals = jnp.sum(jnp.where(hit, weight, 0.0), axis=0, keepdims=True)
        sent_ref[o, NREG:, :] = jnp.where(place == 0, totals, jnp.where(place == 1, energy_total, 0.0))


def elements(rows, cols, density, weight, owner, region, k, ul, x1, x2, y1, y2):
    return pl.pallas_call(
        element_kernel,
        out_shape=jax.ShapeDtypeStruct((OWNERS, SENT_ROWS, LANES), F32),
        in_specs=[SMEM, SMEM] + [VMEM] * 10,
        out_specs=VMEM,
        scratch_shapes=[pltpu.VMEM((NT, BS, LANES), BF16), pltpu.VMEM((NT * 8, LANES), F32), pltpu.VMEM((NT * 8, LANES), F32)],
        compiler_params=PARAMS,
    )(rows, cols, density.reshape(1, NT), weight.reshape(1, NT), owner.reshape(1, NT), region.reshape(1, NT),
      k, ul, x1, x2, y1, y2)


def region_kernel(got_ref, out_ref, energy_ref):
    total = got_ref[0]
    for s in range(1, OWNERS):
        total = total + got_ref[s]
    weights = total[NREG:NREG + 1, :NREG]
    eye = lax.broadcasted_iota(jnp.int32, (NREG, NREG), 0) == lax.broadcasted_iota(jnp.int32, (NREG, NREG), 1)
    divisor = jnp.sum(jnp.where(eye, weights, 0.0), axis=1, keepdims=True)
    out_ref[...] = total[:NREG, :] / jnp.maximum(divisor, 1.0)
    energy = total[NREG + 1:NREG + 2, :]
    energy_ref[...] = jnp.broadcast_to(energy, (energy_ref.shape[0], LANES)).reshape(energy_ref.shape)


def regions(got, columns):
    return pl.pallas_call(
        region_kernel,
        out_shape=[jax.ShapeDtypeStruct((NREG, LANES), F32), jax.ShapeDtypeStruct((columns, 1, LANES), F32)],
        in_specs=[VMEM],
        out_specs=[VMEM, VMEM],
        compiler_params=PARAMS,
    )(got)


def last_kernel(scale, got_ref, out_ref):
    out_ref[...] = (jnp.sum(got_ref[...], axis=0) / scale).reshape(LANES)[:R]


def last(got, scale):
    return pl.pallas_call(
        functools.partial(last_kernel, scale),
        out_shape=jax.ShapeDtypeStruct((R,), F32),
        in_specs=[VMEM],
        out_specs=VMEM,
        compiler_params=PARAMS,
    )(got)


def swaps(axes, size):
    for start in (0, 1):
        firsts = range(start, size - 1, 2)
        yield axes, [(i, i + 1) for i in firsts] + [(i + 1, i) for i in firsts]


def exchange(x, axes):
    return lax.all_to_all(x, axes, split_axis=0, concat_axis=0, tiled=True)


def shards(disp, adjoint, tiles, tile_rows, tile_cols, density, filter_weight, owner, region, face_x, face_y):
    ny, nz, nx, nc = (lax.axis_size(a) for a in ("y", "z", "x", "c"))
    ul, *faces = pack(face_x, face_y, disp, adjoint)
    plans = [*swaps(("y", "z"), ny * nz), *swaps(("x", "c"), nx * nc)]
    halos = [lax.ppermute(face, axes, pairs) for face, (axes, pairs) in zip(faces, plans)]
    k = stiffness(tiles)
    sent = elements(tile_rows, tile_cols, density, filter_weight, owner, region, k, ul, *halos)
    filtered, energy = regions(exchange(sent, ("x", "c")), ny * nz)
    compliance = last(exchange(energy, ("y", "z")), math.sqrt(NT * ny * nz * nx * nc))
    return (filtered, compliance)


def solution(mesh):
    columns, rows = mesh.devices.shape
    nz = 12 if columns % 12 == 0 else columns
    parts = Mesh(mesh.devices.reshape(columns // nz, nz, rows // 2, 2), ("y", "z", "x", "c"))
    axes = ("y", "z", "x", "c")
    flat, wide, deep = P(axes), P(axes, None), P(axes, None, None)
    placed = (wide, wide, wide, flat, flat, flat, flat, wide, flat, deep, deep)
    return jax.shard_map(shards, mesh=parts, in_specs=placed, out_specs=(wide, P()), check_vma=False)
```

```python
import functools
import math

import jax
import jax.numpy as jnp
from jax import lax
from jax.experimental import pallas as pl
from jax.experimental.pallas import tpu as pltpu
from jax.sharding import Mesh, PartitionSpec as P

BS = 64
R = 64
NREG = 32
NB = 64
NT = 96
NIX = 12
NIY = 4
OWNERS = 8
LANES = 128
HALF = BS // 2
SENT_ROWS = 40
GROUP = 32
F32 = jnp.float32
BF16 = jnp.bfloat16
SMEM = pl.BlockSpec(memory_space=pltpu.SMEM)
VMEM = pl.BlockSpec(memory_space=pltpu.VMEM)
HBM = pl.BlockSpec(memory_space=pltpu.HBM)
PARAMS = pltpu.CompilerParams(vmem_limit_bytes=16 << 20)


def pack_kernel(fx_ref, fy_ref, disp_ref, adj_ref, ul_ref, x2_ref, x1_ref, y2_ref, y1_ref, disp, adj, fx, fy, sems):
    pairs = ((disp_ref, disp), (adj_ref, adj), (fx_ref, fx), (fy_ref, fy))
    copies = [pltpu.make_async_copy(src, dst, sems.at[i]) for i, (src, dst) in enumerate(pairs)]
    for copy in copies:
        copy.start()
    for copy in copies:
        copy.wait()
    u = disp[...].reshape(NB, HALF, LANES)
    v = adj[...].reshape(NB, HALF, LANES)
    ul_ref[:, :HALF, :] = jnp.concatenate([u[..., :R], v[..., :R]], axis=-1)
    ul_ref[:, HALF:, :] = jnp.concatenate([u[..., R:], v[..., R:]], axis=-1)
    odd_x = lax.rem(lax.axis_index("z"), 2)
    odd_y = lax.axis_index("c")
    for out, idx, side, count in ((x1_ref, fx, odd_x, NIX), (x2_ref, fx, 1 - odd_x, NIX),
                                  (y1_ref, fy, odd_y, NIY), (y2_ref, fy, 1 - odd_y, NIY)):
        for i in range(count):
            out[i] = ul_ref[idx[0, side, i]]


def pack(face_x, face_y, disp, adjoint):
    args = [pltpu.with_memory_space_constraint(a, pltpu.HBM) for a in (face_x, face_y, disp, adjoint)]
    return pl.pallas_call(
        pack_kernel,
        out_shape=[jax.ShapeDtypeStruct((n, BS, LANES), BF16) for n in (NB, NIX, NIX, NIY, NIY)],
        in_specs=[HBM] * 4,
        out_specs=[VMEM] * 5,
        scratch_shapes=[pltpu.VMEM((NB, BS * R), BF16), pltpu.VMEM((NB, BS * R), BF16),
                        pltpu.SMEM((1, 2, NIX), jnp.int32), pltpu.SMEM((1, 2, NIY), jnp.int32),
                        pltpu.SemaphoreType.DMA((4,))],
        compiler_params=PARAMS,
    )(*args)


def stiffness_kernel(tiles_ref, k_ref):
    pairs = tiles_ref[...].reshape(NT * HALF, LANES)
    source = lax.broadcasted_iota(jnp.int32, (LANES, 2 * LANES), 0)
    target = lax.broadcasted_iota(jnp.int32, (LANES, 2 * LANES), 1)
    lane = target % LANES
    wanted = (target // LANES) * BS + 2 * (lane % HALF) + lane // HALF
    order = ((source == wanted) & (lane < BS)).astype(F32).astype(BF16)
    moved = jnp.dot(pairs, order, preferred_element_type=F32).astype(BF16)
    k_ref[:, :HALF, :] = moved[:, :LANES].reshape(NT, HALF, LANES)
    k_ref[:, HALF:, :] = moved[:, LANES:].reshape(NT, HALF, LANES)


def stiffness(tiles):
    return pl.pallas_call(
        stiffness_kernel,
        out_shape=jax.ShapeDtypeStruct((NT, BS, LANES), BF16),
        in_specs=[VMEM],
        out_specs=VMEM,
        compiler_params=PARAMS,
        cost_estimate=pl.CostEstimate(flops=0, bytes_accessed=8 << 20, transcendentals=0),
    )(tiles)


def column(row):
    return jnp.broadcast_to(row, (LANES, NT)).T


def element_kernel(rows_ref, cols_ref, density_ref, weight_ref, owner_ref, region_ref, k_ref, ul_ref,
                   x2_ref, x1_ref, y2_ref, y1_ref, sent_ref, ext, same8, cross8):
    odd_x = lax.rem(lax.axis_index("z"), 2)
    odd_y = lax.axis_index("c")
    ext[:NB] = ul_ref[...]
    ext[pl.ds(NB + NIX * (1 - odd_x), NIX)] = x1_ref[...]
    ext[pl.ds(NB + NIX * odd_x, NIX)] = x2_ref[...]
    ext[pl.ds(NB + 2 * NIX + NIY * (1 - odd_y), NIY)] = y1_ref[...]
    ext[pl.ds(NB + 2 * NIX + NIY * odd_y, NIY)] = y2_ref[...]

    def body(g, carry):
        for i in range(GROUP):
            t = g * GROUP + i
            row = ul_ref[rows_ref[t]].astype(F32)
            prod = jnp.dot(k_ref[t][:, :BS], ext[cols_ref[t]], preferred_element_type=F32)
            at = pl.ds(pl.multiple_of(t * 8, 8), 8)
            same8[at, :] = jnp.sum((row * prod).reshape(8, 8, LANES), axis=0)
            cross8[at, :] = jnp.sum((pltpu.roll(row, R, 1) * prod).reshape(8, 8, LANES), axis=0)
        return carry

    lax.fori_loop(0, NT // GROUP, body, 0)
    same = same8[pl.ds(0, NT, stride=8), :]
    cross = cross8[pl.ds(0, NT, stride=8), :]
    for s in range(1, 8):
        same = same + same8[pl.ds(s, NT, stride=8), :]
        cross = cross + cross8[pl.ds(s, NT, stride=8), :]
    energy = same / math.sqrt(BS)
    cross = cross + pltpu.roll(cross, R, 1)
    energy_total = jnp.sum(energy, axis=0, keepdims=True)
    rho = column(density_ref[...])
    weight = column(weight_ref[...])
    sens = -(3.0 * rho * rho / (2.0 * math.sqrt(BS))) * cross
    left = lax.broadcasted_iota(jnp.int32, (NT, LANES), 1) < R
    payload = weight * jnp.where(left, sens, pltpu.roll(energy, R, 1))
    ident = owner_ref[...] * NREG + region_ref[...]
    onehot = (lax.broadcasted_iota(jnp.int32, (OWNERS * NREG, NT), 0) == ident).astype(F32).astype(BF16)
    high = payload.astype(BF16)
    rest = payload - high.astype(F32)
    mid = rest.astype(BF16)
    low = (rest - mid.astype(F32)).astype(BF16)
    sums = (jnp.dot(onehot, high, preferred_element_type=F32)
            + jnp.dot(onehot, mid, preferred_element_type=F32)
            + jnp.dot(onehot, low, preferred_element_type=F32))
    ident_column = column(ident.astype(F32)).astype(jnp.int32)
    lane = lax.broadcasted_iota(jnp.int32, (NT, LANES), 1)
    place = lax.broadcasted_iota(jnp.int32, (8, LANES), 0)
    for o in range(OWNERS):
        sent_ref[o, :NREG, :] = sums[o * NREG:(o + 1) * NREG, :]
        hit = (ident_column == lane + o * NREG) & (lane < NREG)
        totals = jnp.sum(jnp.where(hit, weight, 0.0), axis=0, keepdims=True)
        sent_ref[o, NREG:, :] = jnp.where(place == 0, totals, jnp.where(place == 1, energy_total, 0.0))


def elements(rows, cols, density, weight, owner, region, k, ul, x2, x1, y2, y1):
    return pl.pallas_call(
        element_kernel,
        out_shape=jax.ShapeDtypeStruct((OWNERS, SENT_ROWS, LANES), F32),
        in_specs=[SMEM, SMEM] + [VMEM] * 10,
        out_specs=VMEM,
        scratch_shapes=[pltpu.VMEM((NT, BS, LANES), BF16), pltpu.VMEM((NT * 8, LANES), F32), pltpu.VMEM((NT * 8, LANES), F32)],
        compiler_params=PARAMS,
    )(rows, cols, density.reshape(1, NT), weight.reshape(1, NT), owner.reshape(1, NT), region.reshape(1, NT),
      k, ul, x2, x1, y2, y1)


def region_kernel(got_ref, out_ref, energy_ref):
    total = got_ref[0]
    for s in range(1, OWNERS):
        total = total + got_ref[s]
    weights = total[NREG:NREG + 1, :NREG]
    eye = lax.broadcasted_iota(jnp.int32, (NREG, NREG), 0) == lax.broadcasted_iota(jnp.int32, (NREG, NREG), 1)
    divisor = jnp.sum(jnp.where(eye, weights, 0.0), axis=1, keepdims=True)
    out_ref[...] = total[:NREG, :] / jnp.maximum(divisor, 1.0)
    energy = total[NREG + 1:NREG + 2, :]
    energy_ref[...] = jnp.broadcast_to(energy, (energy_ref.shape[0], LANES)).reshape(energy_ref.shape)


def regions(got, columns):
    return pl.pallas_call(
        region_kernel,
        out_shape=[jax.ShapeDtypeStruct((NREG, LANES), F32), jax.ShapeDtypeStruct((columns, 1, LANES), F32)],
        in_specs=[VMEM],
        out_specs=[VMEM, VMEM],
        compiler_params=PARAMS,
    )(got)


def last_kernel(scale, got_ref, out_ref):
    out_ref[...] = (jnp.sum(got_ref[...], axis=0) / scale).reshape(LANES)[:R]


def last(got, scale):
    return pl.pallas_call(
        functools.partial(last_kernel, scale),
        out_shape=jax.ShapeDtypeStruct((R,), F32),
        in_specs=[VMEM],
        out_specs=VMEM,
        compiler_params=PARAMS,
    )(got)


def swaps(axes, size):
    for start in (1, 0):
        firsts = range(start, size - 1, 2)
        yield axes, [(i, i + 1) for i in firsts] + [(i + 1, i) for i in firsts]


def exchange(x, axes):
    return lax.all_to_all(x, axes, split_axis=0, concat_axis=0, tiled=True)


def shards(disp, adjoint, tiles, tile_rows, tile_cols, density, filter_weight, owner, region, face_x, face_y):
    ny, nz, nx, nc = (lax.axis_size(a) for a in ("y", "z", "x", "c"))
    ul, *faces = pack(face_x, face_y, disp, adjoint)
    plans = [*swaps(("y", "z"), ny * nz), *swaps(("x", "c"), nx * nc)]
    halos = [lax.ppermute(face, axes, pairs) for face, (axes, pairs) in zip(faces, plans)]
    k = stiffness(tiles)
    sent = elements(tile_rows, tile_cols, density, filter_weight, owner, region, k, ul, *halos)
    filtered, energy = regions(exchange(sent, ("x", "c")), ny * nz)
    compliance = last(exchange(energy, ("y", "z")), math.sqrt(NT * ny * nz * nx * nc))
    return (filtered, compliance)


def solution(mesh):
    columns, rows = mesh.devices.shape
    nz = 12 if columns % 12 == 0 else columns
    parts = Mesh(mesh.devices.reshape(columns // nz, nz, rows // 2, 2), ("y", "z", "x", "c"))
    axes = ("y", "z", "x", "c")
    flat, wide, deep = P(axes), P(axes, None), P(axes, None, None)
    placed = (wide, wide, wide, flat, flat, flat, flat, wide, flat, deep, deep)
    return jax.shard_map(shards, mesh=parts, in_specs=placed, out_specs=(wide, P()), check_vma=False)
```

```python
import functools
import math

import jax
import jax.numpy as jnp
from jax import lax
from jax.experimental import pallas as pl
from jax.experimental.pallas import tpu as pltpu
from jax.sharding import Mesh, PartitionSpec as P

BS = 64
R = 64
NREG = 32
NB = 64
NT = 96
NIX = 12
NIY = 4
OWNERS = 8
LANES = 128
HALF = BS // 2
SENT_ROWS = 40
GROUP = 32
F32 = jnp.float32
BF16 = jnp.bfloat16
VMEM = pl.BlockSpec(memory_space=pltpu.VMEM)
HBM = pl.BlockSpec(memory_space=pltpu.HBM)
PARAMS = pltpu.CompilerParams(vmem_limit_bytes=16 << 20)


def pack_kernel(fx_ref, fy_ref, disp_ref, adj_ref, ul_ref, x2_ref, x1_ref, y2_ref, y1_ref, disp, adj, fx, fy, sems):
    half = NB // 2
    spans = (slice(0, half), slice(half, NB))
    pairs = [(ref.at[span], buf.at[span]) for span in spans for ref, buf in ((disp_ref, disp), (adj_ref, adj))]
    pairs += [(fx_ref, fx), (fy_ref, fy)]
    copies = [pltpu.make_async_copy(src, dst, sems.at[i]) for i, (src, dst) in enumerate(pairs)]
    for copy in copies:
        copy.start()
    for i, span in enumerate(spans):
        copies[2 * i].wait()
        copies[2 * i + 1].wait()
        u = disp[span, :].reshape(half, HALF, LANES)
        v = adj[span, :].reshape(half, HALF, LANES)
        ul_ref[span, :HALF, :] = jnp.concatenate([u[..., :R], v[..., :R]], axis=-1)
        ul_ref[span, HALF:, :] = jnp.concatenate([u[..., R:], v[..., R:]], axis=-1)
    copies[4].wait()
    copies[5].wait()
    odd_x = lax.rem(lax.axis_index("z"), 2)
    odd_y = lax.axis_index("c")
    for out, idx, side, count in ((x1_ref, fx, odd_x, NIX), (x2_ref, fx, 1 - odd_x, NIX),
                                  (y1_ref, fy, odd_y, NIY), (y2_ref, fy, 1 - odd_y, NIY)):
        for i in range(count):
            out[i] = ul_ref[idx[0, side, i]]


def pack(face_x, face_y, disp, adjoint):
    args = [pltpu.with_memory_space_constraint(a, pltpu.HBM) for a in (face_x, face_y, disp, adjoint)]
    return pl.pallas_call(
        pack_kernel,
        out_shape=[jax.ShapeDtypeStruct((n, BS, LANES), BF16) for n in (NB, NIX, NIX, NIY, NIY)],
        in_specs=[HBM] * 4,
        out_specs=[VMEM] * 5,
        scratch_shapes=[pltpu.VMEM((NB, BS * R), BF16), pltpu.VMEM((NB, BS * R), BF16),
                        pltpu.SMEM((1, 2, NIX), jnp.int32), pltpu.SMEM((1, 2, NIY), jnp.int32),
                        pltpu.SemaphoreType.DMA((6,))],
        compiler_params=PARAMS,
    )(*args)


def stiffness_kernel(tiles_ref, k_ref):
    pairs = tiles_ref[...].reshape(NT * HALF, LANES)
    source = lax.broadcasted_iota(jnp.int32, (LANES, 2 * LANES), 0)
    target = lax.broadcasted_iota(jnp.int32, (LANES, 2 * LANES), 1)
    lane = target % LANES
    wanted = (target // LANES) * BS + 2 * (lane % HALF) + lane // HALF
    order = ((source == wanted) & (lane < BS)).astype(F32).astype(BF16)
    moved = jnp.dot(pairs, order, preferred_element_type=F32).astype(BF16)
    k_ref[:, :HALF, :] = moved[:, :LANES].reshape(NT, HALF, LANES)
    k_ref[:, HALF:, :] = moved[:, LANES:].reshape(NT, HALF, LANES)


def stiffness(tiles):
    return pl.pallas_call(
        stiffness_kernel,
        out_shape=jax.ShapeDtypeStruct((NT, BS, LANES), BF16),
        in_specs=[VMEM],
        out_specs=VMEM,
        compiler_params=PARAMS,
        cost_estimate=pl.CostEstimate(flops=0, bytes_accessed=8 << 20, transcendentals=0),
    )(tiles)


def column(row):
    return jnp.broadcast_to(row, (LANES, NT)).T


def element_kernel(rows_ref, cols_ref, density_ref, weight_ref, owner_ref, region_ref, k_ref, ul_ref,
                   x2_ref, x1_ref, y2_ref, y1_ref, sent_ref, rows, cols, ext, same8, cross8, sems):
    copies = [pltpu.make_async_copy(src, dst, sems.at[i]) for i, (src, dst) in enumerate(((rows_ref, rows), (cols_ref, cols)))]
    for copy in copies:
        copy.start()
    odd_x = lax.rem(lax.axis_index("z"), 2)
    odd_y = lax.axis_index("c")
    ext[:NB] = ul_ref[...]
    ext[pl.ds(NB + NIX * (1 - odd_x), NIX)] = x1_ref[...]
    ext[pl.ds(NB + NIX * odd_x, NIX)] = x2_ref[...]
    ext[pl.ds(NB + 2 * NIX + NIY * (1 - odd_y), NIY)] = y1_ref[...]
    ext[pl.ds(NB + 2 * NIX + NIY * odd_y, NIY)] = y2_ref[...]
    weight = column(weight_ref[...])
    ident = owner_ref[...] * NREG + region_ref[...]
    ident_column = column(ident.astype(F32)).astype(jnp.int32)
    lane = lax.broadcasted_iota(jnp.int32, (NT, LANES), 1)
    place = lax.broadcasted_iota(jnp.int32, (8, LANES), 0)
    for o in range(OWNERS):
        hit = (ident_column == lane + o * NREG) & (lane < NREG)
        totals = jnp.sum(jnp.where(hit, weight, 0.0), axis=0, keepdims=True)
        sent_ref[o, NREG:, :] = jnp.where(place == 0, totals, 0.0)
    for copy in copies:
        copy.wait()

    def body(g, carry):
        for i in range(GROUP):
            t = g * GROUP + i
            row = ul_ref[rows[t]].astype(F32)
            prod = jnp.dot(k_ref[t][:, :BS], ext[cols[t]], preferred_element_type=F32)
            at = pl.ds(pl.multiple_of(t * 8, 8), 8)
            same8[at, :] = jnp.sum((row * prod).reshape(8, 8, LANES), axis=0)
            cross8[at, :] = jnp.sum((pltpu.roll(row, R, 1) * prod).reshape(8, 8, LANES), axis=0)
        return carry

    lax.fori_loop(0, NT // GROUP, body, 0)
    same = same8[pl.ds(0, NT, stride=8), :]
    cross = cross8[pl.ds(0, NT, stride=8), :]
    for s in range(1, 8):
        same = same + same8[pl.ds(s, NT, stride=8), :]
        cross = cross + cross8[pl.ds(s, NT, stride=8), :]
    energy = same / math.sqrt(BS)
    cross = cross + pltpu.roll(cross, R, 1)
    energy_total = jnp.sum(energy, axis=0, keepdims=True)
    rho = column(density_ref[...])
    sens = -(3.0 * rho * rho / (2.0 * math.sqrt(BS))) * cross
    left = lax.broadcasted_iota(jnp.int32, (NT, LANES), 1) < R
    payload = weight * jnp.where(left, sens, pltpu.roll(energy, R, 1))
    onehot = (lax.broadcasted_iota(jnp.int32, (OWNERS * NREG, NT), 0) == ident).astype(F32).astype(BF16)
    high = payload.astype(BF16)
    rest = payload - high.astype(F32)
    mid = rest.astype(BF16)
    low = (rest - mid.astype(F32)).astype(BF16)
    sums = (jnp.dot(onehot, high, preferred_element_type=F32)
            + jnp.dot(onehot, mid, preferred_element_type=F32)
            + jnp.dot(onehot, low, preferred_element_type=F32))
    for o in range(OWNERS):
        sent_ref[o, :NREG, :] = sums[o * NREG:(o + 1) * NREG, :]
        sent_ref[o, NREG + 1:NREG + 2, :] = energy_total


def elements(rows, cols, density, weight, owner, region, k, ul, x2, x1, y2, y1):
    return pl.pallas_call(
        element_kernel,
        out_shape=jax.ShapeDtypeStruct((OWNERS, SENT_ROWS, LANES), F32),
        in_specs=[VMEM] * 12,
        out_specs=VMEM,
        scratch_shapes=[pltpu.SMEM((NT,), jnp.int32), pltpu.SMEM((NT,), jnp.int32), pltpu.VMEM((NT, BS, LANES), BF16),
                        pltpu.VMEM((NT * 8, LANES), F32), pltpu.VMEM((NT * 8, LANES), F32), pltpu.SemaphoreType.DMA((2,))],
        compiler_params=PARAMS,
    )(rows, cols, density.reshape(1, NT), weight.reshape(1, NT), owner.reshape(1, NT), region.reshape(1, NT),
      k, ul, x2, x1, y2, y1)


def region_kernel(got_ref, out_ref, energy_ref):
    total = got_ref[0]
    for s in range(1, OWNERS):
        total = total + got_ref[s]
    weights = total[NREG:NREG + 1, :NREG]
    eye = lax.broadcasted_iota(jnp.int32, (NREG, NREG), 0) == lax.broadcasted_iota(jnp.int32, (NREG, NREG), 1)
    divisor = jnp.sum(jnp.where(eye, weights, 0.0), axis=1, keepdims=True)
    out_ref[...] = total[:NREG, :] / jnp.maximum(divisor, 1.0)
    energy = total[NREG + 1:NREG + 2, :]
    energy_ref[...] = jnp.broadcast_to(energy, (energy_ref.shape[0], LANES)).reshape(energy_ref.shape)


def regions(got, columns):
    return pl.pallas_call(
        region_kernel,
        out_shape=[jax.ShapeDtypeStruct((NREG, LANES), F32), jax.ShapeDtypeStruct((columns, 1, LANES), F32)],
        in_specs=[VMEM],
        out_specs=[VMEM, VMEM],
        compiler_params=PARAMS,
    )(got)


def last_kernel(scale, got_ref, out_ref):
    out_ref[...] = (jnp.sum(got_ref[...], axis=0) / scale).reshape(LANES)[:R]


def last(got, scale):
    return pl.pallas_call(
        functools.partial(last_kernel, scale),
        out_shape=jax.ShapeDtypeStruct((R,), F32),
        in_specs=[VMEM],
        out_specs=VMEM,
        compiler_params=PARAMS,
    )(got)


def swaps(axes, size):
    for start in (1, 0):
        firsts = range(start, size - 1, 2)
        yield axes, [(i, i + 1) for i in firsts] + [(i + 1, i) for i in firsts]


def exchange(x, axes):
    return lax.all_to_all(x, axes, split_axis=0, concat_axis=0, tiled=True)


def shards(disp, adjoint, tiles, tile_rows, tile_cols, density, filter_weight, owner, region, face_x, face_y):
    ny, nz, nx, nc = (lax.axis_size(a) for a in ("y", "z", "x", "c"))
    ul, *faces = pack(face_x, face_y, disp, adjoint)
    plans = [*swaps(("y", "z"), ny * nz), *swaps(("x", "c"), nx * nc)]
    halos = [lax.ppermute(face, axes, pairs) for face, (axes, pairs) in zip(faces, plans)]
    k = stiffness(tiles)
    sent = elements(tile_rows, tile_cols, density, filter_weight, owner, region, k, ul, *halos)
    filtered, energy = regions(exchange(sent, ("x", "c")), ny * nz)
    compliance = last(exchange(energy, ("y", "z")), math.sqrt(NT * ny * nz * nx * nc))
    return (filtered, compliance)


def solution(mesh):
    columns, rows = mesh.devices.shape
    nz = 12 if columns % 12 == 0 else columns
    parts = Mesh(mesh.devices.reshape(columns // nz, nz, rows // 2, 2), ("y", "z", "x", "c"))
    axes = ("y", "z", "x", "c")
    flat, wide, deep = P(axes), P(axes, None), P(axes, None, None)
    placed = (wide, wide, wide, flat, flat, flat, flat, wide, flat, deep, deep)
    return jax.shard_map(shards, mesh=parts, in_specs=placed, out_specs=(wide, P()), check_vma=False)
```

```python
import functools
import math

import jax
import jax.numpy as jnp
from jax import lax
from jax.experimental import pallas as pl
from jax.experimental.pallas import tpu as pltpu
from jax.sharding import Mesh, PartitionSpec as P

BS = 64
R = 64
NREG = 32
NB = 64
NT = 96
NIX = 12
NIY = 4
OWNERS = 8
LANES = 128
HALF = BS // 2
SENT_ROWS = 40
GROUP = 48
F32 = jnp.float32
BF16 = jnp.bfloat16
VMEM = pl.BlockSpec(memory_space=pltpu.VMEM)
HBM = pl.BlockSpec(memory_space=pltpu.HBM)
PARAMS = pltpu.CompilerParams(vmem_limit_bytes=16 << 20)


def pack_kernel(fx_ref, fy_ref, disp_ref, adj_ref, density_ref, weight_ref, owner_ref, region_ref,
                ul_ref, x2_ref, x1_ref, y2_ref, y1_ref, density, weight, owner, region, disp, adj, fx, fy, sems):
    half = NB // 2
    spans = (slice(0, half), slice(half, NB))
    pairs = [(ref.at[span], buf.at[span]) for span in spans for ref, buf in ((disp_ref, disp), (adj_ref, adj))]
    pairs += [(fx_ref, fx), (fy_ref, fy)]
    pairs += [(density_ref, density), (weight_ref, weight), (owner_ref, owner), (region_ref, region)]
    copies = [pltpu.make_async_copy(src, dst, sems.at[i]) for i, (src, dst) in enumerate(pairs)]
    for copy in copies:
        copy.start()
    for i, span in enumerate(spans):
        copies[2 * i].wait()
        copies[2 * i + 1].wait()
        u = disp[span, :].reshape(half, HALF, LANES)
        v = adj[span, :].reshape(half, HALF, LANES)
        ul_ref[span, :HALF, :] = jnp.concatenate([u[..., :R], v[..., :R]], axis=-1)
        ul_ref[span, HALF:, :] = jnp.concatenate([u[..., R:], v[..., R:]], axis=-1)
    copies[4].wait()
    copies[5].wait()
    odd_x = lax.rem(lax.axis_index("z"), 2)
    odd_y = lax.axis_index("c")
    for out, idx, side, count in ((x1_ref, fx, odd_x, NIX), (x2_ref, fx, 1 - odd_x, NIX),
                                  (y1_ref, fy, odd_y, NIY), (y2_ref, fy, 1 - odd_y, NIY)):
        for i in range(count):
            out[i] = ul_ref[idx[0, side, i]]
    for copy in copies[6:]:
        copy.wait()


def pack(*args):
    args = [pltpu.with_memory_space_constraint(a, pltpu.HBM) for a in args]
    return pl.pallas_call(
        pack_kernel,
        out_shape=[jax.ShapeDtypeStruct((n, BS, LANES), BF16) for n in (NB, NIX, NIX, NIY, NIY)]
        + [jax.ShapeDtypeStruct((1, NT), kind) for kind in (F32, F32, jnp.int32, jnp.int32)],
        in_specs=[HBM] * 8,
        out_specs=[VMEM] * 9,
        scratch_shapes=[pltpu.VMEM((NB, BS * R), BF16), pltpu.VMEM((NB, BS * R), BF16),
                        pltpu.SMEM((1, 2, NIX), jnp.int32), pltpu.SMEM((1, 2, NIY), jnp.int32),
                        pltpu.SemaphoreType.DMA((10,))],
        compiler_params=PARAMS,
    )(*args)


def column(row):
    return jnp.broadcast_to(row, (LANES, NT)).T


def stiffness_kernel(density_ref, weight_ref, owner_ref, region_ref, tiles_ref, k_ref, factor_ref, wide_ref, totals_ref):
    pairs = tiles_ref[...].reshape(NT * HALF, LANES)
    source = lax.broadcasted_iota(jnp.int32, (LANES, 2 * LANES), 0)
    target = lax.broadcasted_iota(jnp.int32, (LANES, 2 * LANES), 1)
    lane = target % LANES
    wanted = (target // LANES) * BS + 2 * (lane % HALF) + lane // HALF
    order = ((source == wanted) & (lane < BS)).astype(F32).astype(BF16)
    moved = jnp.dot(pairs, order, preferred_element_type=F32).astype(BF16)
    k_ref[:, :HALF, :] = moved[:, :LANES].reshape(NT, HALF, LANES)
    k_ref[:, HALF:, :] = moved[:, LANES:].reshape(NT, HALF, LANES)
    rho = column(density_ref[...])
    factor_ref[...] = -(3.0 * rho * rho / (2.0 * math.sqrt(BS)))
    weight = column(weight_ref[...])
    wide_ref[...] = weight
    ident = column((owner_ref[...] * NREG + region_ref[...]).astype(F32)).astype(jnp.int32)
    lane = lax.broadcasted_iota(jnp.int32, (NT, LANES), 1)
    place = lax.broadcasted_iota(jnp.int32, (8, LANES), 0)
    for o in range(OWNERS):
        hit = (ident == lane + o * NREG) & (lane < NREG)
        totals = jnp.sum(jnp.where(hit, weight, 0.0), axis=0, keepdims=True)
        totals_ref[o] = jnp.where(place == 0, totals, 0.0)


def stiffness(density, weight, owner, region, tiles):
    return pl.pallas_call(
        stiffness_kernel,
        out_shape=[jax.ShapeDtypeStruct((NT, BS, LANES), BF16), jax.ShapeDtypeStruct((NT, LANES), F32),
                   jax.ShapeDtypeStruct((NT, LANES), F32), jax.ShapeDtypeStruct((OWNERS, 8, LANES), F32)],
        in_specs=[VMEM] * 5,
        out_specs=[VMEM] * 4,
        compiler_params=PARAMS,
        cost_estimate=pl.CostEstimate(flops=0, bytes_accessed=8 << 20, transcendentals=0),
    )(density, weight, owner, region, tiles)


def element_kernel(rows_ref, cols_ref, owner_ref, region_ref, k_ref, factor_ref, wide_ref, totals_ref, ul_ref,
                   x2_ref, x1_ref, y2_ref, y1_ref, sent_ref, rows, cols, ext, same8, cross8, sems):
    copies = [pltpu.make_async_copy(src, dst, sems.at[i]) for i, (src, dst) in enumerate(((rows_ref, rows), (cols_ref, cols)))]
    for copy in copies:
        copy.start()
    odd_x = lax.rem(lax.axis_index("z"), 2)
    odd_y = lax.axis_index("c")
    ext[:NB] = ul_ref[...]
    ext[pl.ds(NB + NIX * (1 - odd_x), NIX)] = x1_ref[...]
    ext[pl.ds(NB + NIX * odd_x, NIX)] = x2_ref[...]
    ext[pl.ds(NB + 2 * NIX + NIY * (1 - odd_y), NIY)] = y1_ref[...]
    ext[pl.ds(NB + 2 * NIX + NIY * odd_y, NIY)] = y2_ref[...]
    for copy in copies:
        copy.wait()

    def body(g, carry):
        for i in range(GROUP):
            t = g * GROUP + i
            row = ul_ref[rows[t]].astype(F32)
            prod = jnp.dot(k_ref[t][:, :BS], ext[cols[t]], preferred_element_type=F32)
            at = pl.ds(pl.multiple_of(t * 8, 8), 8)
            same8[at, :] = jnp.sum((row * prod).reshape(8, 8, LANES), axis=0)
            cross8[at, :] = jnp.sum((pltpu.roll(row, R, 1) * prod).reshape(8, 8, LANES), axis=0)
        return carry

    lax.fori_loop(0, NT // GROUP, body, 0)
    same = same8[pl.ds(0, NT, stride=8), :]
    cross = cross8[pl.ds(0, NT, stride=8), :]
    for s in range(1, 8):
        same = same + same8[pl.ds(s, NT, stride=8), :]
        cross = cross + cross8[pl.ds(s, NT, stride=8), :]
    energy = same / math.sqrt(BS)
    cross = cross + pltpu.roll(cross, R, 1)
    energy_total = jnp.sum(energy, axis=0, keepdims=True)
    sens = factor_ref[...] * cross
    left = lax.broadcasted_iota(jnp.int32, (NT, LANES), 1) < R
    payload = wide_ref[...] * jnp.where(left, sens, pltpu.roll(energy, R, 1))
    ident = owner_ref[...] * NREG + region_ref[...]
    onehot = (lax.broadcasted_iota(jnp.int32, (OWNERS * NREG, NT), 0) == ident).astype(F32).astype(BF16)
    high = payload.astype(BF16)
    rest = payload - high.astype(F32)
    mid = rest.astype(BF16)
    low = (rest - mid.astype(F32)).astype(BF16)
    sums = (jnp.dot(onehot, high, preferred_element_type=F32)
            + jnp.dot(onehot, mid, preferred_element_type=F32)
            + jnp.dot(onehot, low, preferred_element_type=F32))
    place = lax.broadcasted_iota(jnp.int32, (8, LANES), 0)
    for o in range(OWNERS):
        sent_ref[o, :NREG, :] = sums[o * NREG:(o + 1) * NREG, :]
        sent_ref[o, NREG:, :] = jnp.where(place == 1, energy_total, totals_ref[o])


def elements(rows, cols, owner, region, k, factor, wide, totals, ul, x2, x1, y2, y1):
    return pl.pallas_call(
        element_kernel,
        out_shape=jax.ShapeDtypeStruct((OWNERS, SENT_ROWS, LANES), F32),
        in_specs=[VMEM] * 13,
        out_specs=VMEM,
        scratch_shapes=[pltpu.SMEM((NT,), jnp.int32), pltpu.SMEM((NT,), jnp.int32), pltpu.VMEM((NT, BS, LANES), BF16),
                        pltpu.VMEM((NT * 8, LANES), F32), pltpu.VMEM((NT * 8, LANES), F32), pltpu.SemaphoreType.DMA((2,))],
        compiler_params=PARAMS,
    )(rows, cols, owner, region, k, factor, wide, totals, ul, x2, x1, y2, y1)


def region_kernel(got_ref, out_ref, energy_ref):
    total = got_ref[0]
    for s in range(1, OWNERS):
        total = total + got_ref[s]
    weights = total[NREG:NREG + 1, :NREG]
    eye = lax.broadcasted_iota(jnp.int32, (NREG, NREG), 0) == lax.broadcasted_iota(jnp.int32, (NREG, NREG), 1)
    divisor = jnp.sum(jnp.where(eye, weights, 0.0), axis=1, keepdims=True)
    out_ref[...] = total[:NREG, :] / jnp.maximum(divisor, 1.0)
    energy = total[NREG + 1:NREG + 2, :]
    energy_ref[...] = jnp.broadcast_to(energy, (energy_ref.shape[0], LANES)).reshape(energy_ref.shape)


def regions(got, columns):
    return pl.pallas_call(
        region_kernel,
        out_shape=[jax.ShapeDtypeStruct((NREG, LANES), F32), jax.ShapeDtypeStruct((columns, 1, LANES), F32)],
        in_specs=[VMEM],
        out_specs=[VMEM, VMEM],
        compiler_params=PARAMS,
    )(got)


def last_kernel(scale, got_ref, out_ref):
    out_ref[...] = (jnp.sum(got_ref[...], axis=0) / scale).reshape(LANES)[:R]


def last(got, scale):
    return pl.pallas_call(
        functools.partial(last_kernel, scale),
        out_shape=jax.ShapeDtypeStruct((R,), F32),
        in_specs=[VMEM],
        out_specs=VMEM,
        compiler_params=PARAMS,
    )(got)


def swaps(axes, size):
    for start in (1, 0):
        firsts = range(start, size - 1, 2)
        yield axes, [(i, i + 1) for i in firsts] + [(i + 1, i) for i in firsts]


def exchange(x, axes):
    return lax.all_to_all(x, axes, split_axis=0, concat_axis=0, tiled=True)


def shards(disp, adjoint, tiles, tile_rows, tile_cols, density, filter_weight, owner, region, face_x, face_y):
    ny, nz, nx, nc = (lax.axis_size(a) for a in ("y", "z", "x", "c"))
    scalars = [a.reshape(1, NT) for a in (density, filter_weight, owner, region)]
    ul, *faces, density, weight, owner, region = pack(face_x, face_y, disp, adjoint, *scalars)
    plans = [*swaps(("y", "z"), ny * nz), *swaps(("x", "c"), nx * nc)]
    halos = [lax.ppermute(face, axes, pairs) for face, (axes, pairs) in zip(faces, plans)]
    k, factor, wide, totals = stiffness(density, weight, owner, region, tiles)
    sent = elements(tile_rows, tile_cols, owner, region, k, factor, wide, totals, ul, *halos)
    filtered, energy = regions(exchange(sent, ("x", "c")), ny * nz)
    compliance = last(exchange(energy, ("y", "z")), math.sqrt(NT * ny * nz * nx * nc))
    return (filtered, compliance)


def solution(mesh):
    columns, rows = mesh.devices.shape
    nz = 12 if columns % 12 == 0 else columns
    parts = Mesh(mesh.devices.reshape(columns // nz, nz, rows // 2, 2), ("y", "z", "x", "c"))
    axes = ("y", "z", "x", "c")
    flat, wide, deep = P(axes), P(axes, None), P(axes, None, None)
    placed = (wide, wide, wide, flat, flat, flat, flat, wide, flat, deep, deep)
    return jax.shard_map(shards, mesh=parts, in_specs=placed, out_specs=(wide, P()), check_vma=False)
```

```python
import functools
import math

import jax
import jax.numpy as jnp
from jax import lax
from jax.experimental import pallas as pl
from jax.experimental.pallas import tpu as pltpu
from jax.sharding import Mesh, PartitionSpec as P

BS = 64
R = 64
NREG = 32
NB = 64
NT = 96
NIX = 12
NIY = 4
OWNERS = 8
LANES = 128
HALF = BS // 2
SENT_ROWS = 40
GROUP = 48
F32 = jnp.float32
BF16 = jnp.bfloat16
VMEM = pl.BlockSpec(memory_space=pltpu.VMEM)
HBM = pl.BlockSpec(memory_space=pltpu.HBM)
PARAMS = pltpu.CompilerParams(vmem_limit_bytes=16 << 20)


def pack_kernel(fx_ref, fy_ref, disp_ref, adj_ref, density_ref, weight_ref, owner_ref, region_ref,
                ul_ref, x2_ref, x1_ref, y2_ref, y1_ref, density, weight, owner, region, disp, adj, fx, fy, sems):
    half = NB // 2
    spans = (slice(0, half), slice(half, NB))
    pairs = [(ref.at[span], buf.at[span]) for span in spans for ref, buf in ((disp_ref, disp), (adj_ref, adj))]
    pairs += [(fx_ref, fx), (fy_ref, fy)]
    pairs += [(density_ref, density), (weight_ref, weight), (owner_ref, owner), (region_ref, region)]
    copies = [pltpu.make_async_copy(src, dst, sems.at[i]) for i, (src, dst) in enumerate(pairs)]
    for copy in copies:
        copy.start()
    for i, span in enumerate(spans):
        copies[2 * i].wait()
        copies[2 * i + 1].wait()
        u = disp[span, :].reshape(half, HALF, LANES)
        v = adj[span, :].reshape(half, HALF, LANES)
        ul_ref[span, :HALF, :] = jnp.concatenate([u[..., :R], v[..., :R]], axis=-1)
        ul_ref[span, HALF:, :] = jnp.concatenate([u[..., R:], v[..., R:]], axis=-1)
    copies[4].wait()
    copies[5].wait()
    odd_x = lax.rem(lax.axis_index("z"), 2)
    odd_y = lax.axis_index("c")
    for out, idx, side, count in ((x1_ref, fx, odd_x, NIX), (x2_ref, fx, 1 - odd_x, NIX),
                                  (y1_ref, fy, odd_y, NIY), (y2_ref, fy, 1 - odd_y, NIY)):
        for i in range(count):
            out[i] = ul_ref[idx[0, side, i]]
    for copy in copies[6:]:
        copy.wait()


def pack(*args):
    args = [pltpu.with_memory_space_constraint(a, pltpu.HBM) for a in args]
    return pl.pallas_call(
        pack_kernel,
        out_shape=[jax.ShapeDtypeStruct((n, BS, LANES), BF16) for n in (NB, NIX, NIX, NIY, NIY)]
        + [jax.ShapeDtypeStruct((1, NT), kind) for kind in (F32, F32, jnp.int32, jnp.int32)],
        in_specs=[HBM] * 8,
        out_specs=[VMEM] * 9,
        scratch_shapes=[pltpu.VMEM((NB, BS * R), BF16), pltpu.VMEM((NB, BS * R), BF16),
                        pltpu.SMEM((1, 2, NIX), jnp.int32), pltpu.SMEM((1, 2, NIY), jnp.int32),
                        pltpu.SemaphoreType.DMA((10,))],
        compiler_params=PARAMS,
    )(*args)


def column(row):
    return jnp.broadcast_to(row, (LANES, NT)).T


def stiffness_kernel(density_ref, weight_ref, owner_ref, region_ref, tiles_ref, k_ref, factor_ref, wide_ref, totals_ref):
    pairs = tiles_ref[...].reshape(NT * HALF, LANES)
    source = lax.broadcasted_iota(jnp.int32, (LANES, 2 * LANES), 0)
    target = lax.broadcasted_iota(jnp.int32, (LANES, 2 * LANES), 1)
    lane = target % LANES
    wanted = (target // LANES) * BS + 2 * (lane % HALF) + lane // HALF
    order = ((source == wanted) & (lane < BS)).astype(F32).astype(BF16)
    moved = jnp.dot(pairs, order, preferred_element_type=F32).astype(BF16)
    k_ref[:, :HALF, :] = moved[:, :LANES].reshape(NT, HALF, LANES)
    k_ref[:, HALF:, :] = moved[:, LANES:].reshape(NT, HALF, LANES)
    rho = column(density_ref[...])
    factor_ref[...] = -(3.0 * rho * rho / (2.0 * math.sqrt(BS)))
    weight = column(weight_ref[...])
    wide_ref[...] = weight
    ident = column((owner_ref[...] * NREG + region_ref[...]).astype(F32)).astype(jnp.int32)
    lane = lax.broadcasted_iota(jnp.int32, (NT, LANES), 1)
    place = lax.broadcasted_iota(jnp.int32, (8, LANES), 0)
    for o in range(OWNERS):
        hit = (ident == lane + o * NREG) & (lane < NREG)
        totals = jnp.sum(jnp.where(hit, weight, 0.0), axis=0, keepdims=True)
        totals_ref[o] = jnp.where(place == 0, totals, 0.0)


def stiffness(density, weight, owner, region, tiles):
    return pl.pallas_call(
        stiffness_kernel,
        out_shape=[jax.ShapeDtypeStruct((NT, BS, LANES), BF16), jax.ShapeDtypeStruct((NT, LANES), F32),
                   jax.ShapeDtypeStruct((NT, LANES), F32), jax.ShapeDtypeStruct((OWNERS, 8, LANES), F32)],
        in_specs=[VMEM] * 5,
        out_specs=[VMEM] * 4,
        compiler_params=PARAMS,
        cost_estimate=pl.CostEstimate(flops=0, bytes_accessed=8 << 20, transcendentals=0),
    )(density, weight, owner, region, tiles)


def element_kernel(rows_ref, cols_ref, owner_ref, region_ref, k_ref, factor_ref, wide_ref, totals_ref, ul_ref,
                   x2_ref, x1_ref, y2_ref, y1_ref, sent_ref, rows, cols, ext, same8, cross8, sems):
    copies = [pltpu.make_async_copy(src, dst, sems.at[i]) for i, (src, dst) in enumerate(((rows_ref, rows), (cols_ref, cols)))]
    for copy in copies:
        copy.start()
    odd_x = lax.rem(lax.axis_index("z"), 2)
    odd_y = lax.axis_index("c")
    ext[:NB] = ul_ref[...]
    ext[pl.ds(NB + NIX * (1 - odd_x), NIX)] = x1_ref[...]
    ext[pl.ds(NB + NIX * odd_x, NIX)] = x2_ref[...]
    ext[pl.ds(NB + 2 * NIX + NIY * (1 - odd_y), NIY)] = y1_ref[...]
    ext[pl.ds(NB + 2 * NIX + NIY * odd_y, NIY)] = y2_ref[...]
    for copy in copies:
        copy.wait()

    def body(g, carry):
        for i in range(GROUP):
            t = g * GROUP + i
            row = ul_ref[rows[t]].astype(F32)
            prod = jnp.dot(k_ref[t][:, :BS], ext[cols[t]], preferred_element_type=F32)
            at = pl.ds(pl.multiple_of(t * 8, 8), 8)
            same8[at, :] = jnp.sum((row * prod).reshape(8, 8, LANES), axis=0)
            cross8[at, :] = jnp.sum((pltpu.roll(row, R, 1) * prod).reshape(8, 8, LANES), axis=0)
        return carry

    lax.fori_loop(0, NT // GROUP, body, 0)
    same = same8[pl.ds(0, NT, stride=8), :]
    cross = cross8[pl.ds(0, NT, stride=8), :]
    for s in range(1, 8):
        same = same + same8[pl.ds(s, NT, stride=8), :]
        cross = cross + cross8[pl.ds(s, NT, stride=8), :]
    energy = same / math.sqrt(BS)
    cross = cross + pltpu.roll(cross, R, 1)
    energy_total = jnp.sum(energy, axis=0, keepdims=True)
    sens = factor_ref[...] * cross
    left = lax.broadcasted_iota(jnp.int32, (NT, LANES), 1) < R
    payload = wide_ref[...] * jnp.where(left, sens, pltpu.roll(energy, R, 1))
    ident = owner_ref[...] * NREG + region_ref[...]
    onehot = (lax.broadcasted_iota(jnp.int32, (OWNERS * NREG, NT), 0) == ident).astype(F32).astype(BF16)
    high = payload.astype(BF16)
    rest = payload - high.astype(F32)
    mid = rest.astype(BF16)
    low = (rest - mid.astype(F32)).astype(BF16)
    sums = (jnp.dot(onehot, high, preferred_element_type=F32)
            + jnp.dot(onehot, mid, preferred_element_type=F32)
            + jnp.dot(onehot, low, preferred_element_type=F32))
    place = lax.broadcasted_iota(jnp.int32, (8, LANES), 0)
    for o in range(OWNERS):
        slot = o % 2 * (OWNERS // 2) + o // 2
        sent_ref[slot, :NREG, :] = sums[o * NREG:(o + 1) * NREG, :]
        sent_ref[slot, NREG:, :] = jnp.where(place == 1, energy_total, totals_ref[o])


def elements(rows, cols, owner, region, k, factor, wide, totals, ul, x2, x1, y2, y1):
    return pl.pallas_call(
        element_kernel,
        out_shape=jax.ShapeDtypeStruct((OWNERS, SENT_ROWS, LANES), F32),
        in_specs=[VMEM] * 13,
        out_specs=VMEM,
        scratch_shapes=[pltpu.SMEM((NT,), jnp.int32), pltpu.SMEM((NT,), jnp.int32), pltpu.VMEM((NT, BS, LANES), BF16),
                        pltpu.VMEM((NT * 8, LANES), F32), pltpu.VMEM((NT * 8, LANES), F32), pltpu.SemaphoreType.DMA((2,))],
        compiler_params=PARAMS,
    )(rows, cols, owner, region, k, factor, wide, totals, ul, x2, x1, y2, y1)


def region_kernel(got_ref, out_ref, energy_ref):
    total = got_ref[0]
    for s in range(1, OWNERS):
        total = total + got_ref[s]
    weights = total[NREG:NREG + 1, :NREG]
    eye = lax.broadcasted_iota(jnp.int32, (NREG, NREG), 0) == lax.broadcasted_iota(jnp.int32, (NREG, NREG), 1)
    divisor = jnp.sum(jnp.where(eye, weights, 0.0), axis=1, keepdims=True)
    out_ref[...] = total[:NREG, :] / jnp.maximum(divisor, 1.0)
    energy = total[NREG + 1:NREG + 2, :]
    energy_ref[...] = jnp.broadcast_to(energy, (energy_ref.shape[0], LANES)).reshape(energy_ref.shape)


def regions(got, columns):
    return pl.pallas_call(
        region_kernel,
        out_shape=[jax.ShapeDtypeStruct((NREG, LANES), F32), jax.ShapeDtypeStruct((columns, 1, LANES), F32)],
        in_specs=[VMEM],
        out_specs=[VMEM, VMEM],
        compiler_params=PARAMS,
    )(got)


def last_kernel(scale, got_ref, out_ref):
    out_ref[...] = (jnp.sum(got_ref[...], axis=0) / scale).reshape(LANES)[:R]


def last(got, scale):
    return pl.pallas_call(
        functools.partial(last_kernel, scale),
        out_shape=jax.ShapeDtypeStruct((R,), F32),
        in_specs=[VMEM],
        out_specs=VMEM,
        compiler_params=PARAMS,
    )(got)


def swaps(axes, size):
    for start in (1, 0):
        firsts = range(start, size - 1, 2)
        yield axes, [(i, i + 1) for i in firsts] + [(i + 1, i) for i in firsts]


def exchange(x, axes):
    return lax.all_to_all(x, axes, split_axis=0, concat_axis=0, tiled=True)


def shards(disp, adjoint, tiles, tile_rows, tile_cols, density, filter_weight, owner, region, face_x, face_y):
    ny, nz, nx, nc = (lax.axis_size(a) for a in ("y", "z", "x", "c"))
    scalars = [a.reshape(1, NT) for a in (density, filter_weight, owner, region)]
    ul, *faces, density, weight, owner, region = pack(face_x, face_y, disp, adjoint, *scalars)
    plans = [*swaps(("y", "z"), ny * nz), *swaps(("x", "c"), nx * nc)]
    halos = [lax.ppermute(face, axes, pairs) for face, (axes, pairs) in zip(faces, plans)]
    k, factor, wide, totals = stiffness(density, weight, owner, region, tiles)
    sent = elements(tile_rows, tile_cols, owner, region, k, factor, wide, totals, ul, *halos)
    filtered, energy = regions(exchange(sent, ("c", "x")), ny * nz)
    compliance = last(exchange(energy, ("y", "z")), math.sqrt(NT * ny * nz * nx * nc))
    return (filtered, compliance)


def solution(mesh):
    columns, rows = mesh.devices.shape
    nz = 12 if columns % 12 == 0 else columns
    parts = Mesh(mesh.devices.reshape(columns // nz, nz, rows // 2, 2), ("y", "z", "x", "c"))
    axes = ("y", "z", "x", "c")
    flat, wide, deep = P(axes), P(axes, None), P(axes, None, None)
    placed = (wide, wide, wide, flat, flat, flat, flat, wide, flat, deep, deep)
    return jax.shard_map(shards, mesh=parts, in_specs=placed, out_specs=(wide, P()), check_vma=False)
```

```python
import functools
import math

import jax
import jax.numpy as jnp
from jax import lax
from jax.experimental import pallas as pl
from jax.experimental.pallas import tpu as pltpu
from jax.sharding import Mesh, PartitionSpec as P

BS = 64
R = 64
NREG = 32
NB = 64
NT = 96
NIX = 12
NIY = 4
OWNERS = 8
LANES = 128
HALF = BS // 2
SENT_ROWS = 40
GROUP = 96
F32 = jnp.float32
BF16 = jnp.bfloat16
VMEM = pl.BlockSpec(memory_space=pltpu.VMEM)
HBM = pl.BlockSpec(memory_space=pltpu.HBM)
PARAMS = pltpu.CompilerParams(vmem_limit_bytes=16 << 20)


def pack_kernel(fx_ref, fy_ref, disp_ref, adj_ref, density_ref, weight_ref, owner_ref, region_ref,
                ul_ref, x2_ref, x1_ref, y2_ref, y1_ref, density, weight, owner, region, disp, adj, fx, fy, sems):
    half = NB // 2
    spans = (slice(0, half), slice(half, NB))
    pairs = [(ref.at[span], buf.at[span]) for span in spans for ref, buf in ((disp_ref, disp), (adj_ref, adj))]
    pairs += [(fx_ref, fx), (fy_ref, fy)]
    pairs += [(density_ref, density), (weight_ref, weight), (owner_ref, owner), (region_ref, region)]
    copies = [pltpu.make_async_copy(src, dst, sems.at[i]) for i, (src, dst) in enumerate(pairs)]
    for copy in copies:
        copy.start()
    for i, span in enumerate(spans):
        copies[2 * i].wait()
        copies[2 * i + 1].wait()
        u = disp[span, :].reshape(half, HALF, LANES)
        v = adj[span, :].reshape(half, HALF, LANES)
        ul_ref[span, :HALF, :] = jnp.concatenate([u[..., :R], v[..., :R]], axis=-1)
        ul_ref[span, HALF:, :] = jnp.concatenate([u[..., R:], v[..., R:]], axis=-1)
    copies[4].wait()
    copies[5].wait()
    odd_x = lax.rem(lax.axis_index("z"), 2)
    odd_y = lax.axis_index("c")
    for out, idx, side, count in ((x1_ref, fx, odd_x, NIX), (x2_ref, fx, 1 - odd_x, NIX),
                                  (y1_ref, fy, odd_y, NIY), (y2_ref, fy, 1 - odd_y, NIY)):
        for i in range(count):
            out[i] = ul_ref[idx[0, side, i]]
    for copy in copies[6:]:
        copy.wait()


def pack(*args):
    args = [pltpu.with_memory_space_constraint(a, pltpu.HBM) for a in args]
    return pl.pallas_call(
        pack_kernel,
        out_shape=[jax.ShapeDtypeStruct((n, BS, LANES), BF16) for n in (NB, NIX, NIX, NIY, NIY)]
        + [jax.ShapeDtypeStruct((1, NT), kind) for kind in (F32, F32, jnp.int32, jnp.int32)],
        in_specs=[HBM] * 8,
        out_specs=[VMEM] * 9,
        scratch_shapes=[pltpu.VMEM((NB, BS * R), BF16), pltpu.VMEM((NB, BS * R), BF16),
                        pltpu.SMEM((1, 2, NIX), jnp.int32), pltpu.SMEM((1, 2, NIY), jnp.int32),
                        pltpu.SemaphoreType.DMA((10,))],
        compiler_params=PARAMS,
    )(*args)


def column(row):
    return jnp.broadcast_to(row, (LANES, NT)).T


def stiffness_kernel(density_ref, weight_ref, owner_ref, region_ref, tiles_ref, k_ref, factor_ref, wide_ref, totals_ref):
    pairs = tiles_ref[...].reshape(NT * HALF, LANES)
    source = lax.broadcasted_iota(jnp.int32, (LANES, 2 * LANES), 0)
    target = lax.broadcasted_iota(jnp.int32, (LANES, 2 * LANES), 1)
    lane = target % LANES
    wanted = (target // LANES) * BS + 2 * (lane % HALF) + lane // HALF
    order = ((source == wanted) & (lane < BS)).astype(F32).astype(BF16)
    moved = jnp.dot(pairs, order, preferred_element_type=F32).astype(BF16)
    k_ref[:, :HALF, :] = moved[:, :LANES].reshape(NT, HALF, LANES)
    k_ref[:, HALF:, :] = moved[:, LANES:].reshape(NT, HALF, LANES)
    rho = column(density_ref[...])
    factor_ref[...] = -(3.0 * rho * rho / (2.0 * math.sqrt(BS)))
    weight = column(weight_ref[...])
    wide_ref[...] = weight
    ident = column((owner_ref[...] * NREG + region_ref[...]).astype(F32)).astype(jnp.int32)
    lane = lax.broadcasted_iota(jnp.int32, (NT, LANES), 1)
    place = lax.broadcasted_iota(jnp.int32, (8, LANES), 0)
    for o in range(OWNERS):
        hit = (ident == lane + o * NREG) & (lane < NREG)
        totals = jnp.sum(jnp.where(hit, weight, 0.0), axis=0, keepdims=True)
        totals_ref[o] = jnp.where(place == 0, totals, 0.0)


def stiffness(density, weight, owner, region, tiles):
    return pl.pallas_call(
        stiffness_kernel,
        out_shape=[jax.ShapeDtypeStruct((NT, BS, LANES), BF16), jax.ShapeDtypeStruct((NT, LANES), F32),
                   jax.ShapeDtypeStruct((NT, LANES), F32), jax.ShapeDtypeStruct((OWNERS, 8, LANES), F32)],
        in_specs=[VMEM] * 5,
        out_specs=[VMEM] * 4,
        compiler_params=PARAMS,
        cost_estimate=pl.CostEstimate(flops=0, bytes_accessed=8 << 20, transcendentals=0),
    )(density, weight, owner, region, tiles)


def element_kernel(rows_ref, cols_ref, owner_ref, region_ref, k_ref, factor_ref, wide_ref, totals_ref, ul_ref,
                   x2_ref, x1_ref, y2_ref, y1_ref, sent_ref, rows, cols, ext, same8, cross8, sems):
    copies = [pltpu.make_async_copy(src, dst, sems.at[i]) for i, (src, dst) in enumerate(((rows_ref, rows), (cols_ref, cols)))]
    for copy in copies:
        copy.start()
    odd_x = lax.rem(lax.axis_index("z"), 2)
    odd_y = lax.axis_index("c")
    ext[:NB] = ul_ref[...]
    ext[pl.ds(NB + NIX * (1 - odd_x), NIX)] = x1_ref[...]
    ext[pl.ds(NB + NIX * odd_x, NIX)] = x2_ref[...]
    ext[pl.ds(NB + 2 * NIX + NIY * (1 - odd_y), NIY)] = y1_ref[...]
    ext[pl.ds(NB + 2 * NIX + NIY * odd_y, NIY)] = y2_ref[...]
    for copy in copies:
        copy.wait()

    def body(g, carry):
        for i in range(GROUP):
            t = g * GROUP + i
            row = ul_ref[rows[t]].astype(F32)
            prod = jnp.dot(k_ref[t][:, :BS], ext[cols[t]], preferred_element_type=F32)
            at = pl.ds(pl.multiple_of(t * 8, 8), 8)
            same8[at, :] = jnp.sum((row * prod).reshape(8, 8, LANES), axis=0)
            cross8[at, :] = jnp.sum((pltpu.roll(row, R, 1) * prod).reshape(8, 8, LANES), axis=0)
        return carry

    lax.fori_loop(0, NT // GROUP, body, 0)
    same = same8[pl.ds(0, NT, stride=8), :]
    cross = cross8[pl.ds(0, NT, stride=8), :]
    for s in range(1, 8):
        same = same + same8[pl.ds(s, NT, stride=8), :]
        cross = cross + cross8[pl.ds(s, NT, stride=8), :]
    energy = same / math.sqrt(BS)
    cross = cross + pltpu.roll(cross, R, 1)
    energy_total = jnp.sum(energy, axis=0, keepdims=True)
    sens = factor_ref[...] * cross
    left = lax.broadcasted_iota(jnp.int32, (NT, LANES), 1) < R
    payload = wide_ref[...] * jnp.where(left, sens, pltpu.roll(energy, R, 1))
    ident = owner_ref[...] * NREG + region_ref[...]
    onehot = (lax.broadcasted_iota(jnp.int32, (OWNERS * NREG, NT), 0) == ident).astype(F32).astype(BF16)
    high = payload.astype(BF16)
    rest = payload - high.astype(F32)
    mid = rest.astype(BF16)
    low = (rest - mid.astype(F32)).astype(BF16)
    sums = (jnp.dot(onehot, high, preferred_element_type=F32)
            + jnp.dot(onehot, mid, preferred_element_type=F32)
            + jnp.dot(onehot, low, preferred_element_type=F32))
    place = lax.broadcasted_iota(jnp.int32, (8, LANES), 0)
    for o in range(OWNERS):
        slot = o % 2 * (OWNERS // 2) + o // 2
        sent_ref[slot, :NREG, :] = sums[o * NREG:(o + 1) * NREG, :]
        sent_ref[slot, NREG:, :] = jnp.where(place == 1, energy_total, totals_ref[o])


def elements(rows, cols, owner, region, k, factor, wide, totals, ul, x2, x1, y2, y1):
    return pl.pallas_call(
        element_kernel,
        out_shape=jax.ShapeDtypeStruct((OWNERS, SENT_ROWS, LANES), F32),
        in_specs=[VMEM] * 13,
        out_specs=VMEM,
        scratch_shapes=[pltpu.SMEM((NT,), jnp.int32), pltpu.SMEM((NT,), jnp.int32), pltpu.VMEM((NT, BS, LANES), BF16),
                        pltpu.VMEM((NT * 8, LANES), F32), pltpu.VMEM((NT * 8, LANES), F32), pltpu.SemaphoreType.DMA((2,))],
        compiler_params=PARAMS,
    )(rows, cols, owner, region, k, factor, wide, totals, ul, x2, x1, y2, y1)


def region_kernel(got_ref, out_ref, energy_ref):
    total = got_ref[0]
    for s in range(1, OWNERS):
        total = total + got_ref[s]
    weights = total[NREG:NREG + 1, :NREG]
    eye = lax.broadcasted_iota(jnp.int32, (NREG, NREG), 0) == lax.broadcasted_iota(jnp.int32, (NREG, NREG), 1)
    divisor = jnp.sum(jnp.where(eye, weights, 0.0), axis=1, keepdims=True)
    out_ref[...] = total[:NREG, :] / jnp.maximum(divisor, 1.0)
    energy = total[NREG + 1:NREG + 2, :]
    energy_ref[...] = jnp.broadcast_to(energy, (energy_ref.shape[0], LANES)).reshape(energy_ref.shape)


def regions(got, columns):
    return pl.pallas_call(
        region_kernel,
        out_shape=[jax.ShapeDtypeStruct((NREG, LANES), F32), jax.ShapeDtypeStruct((columns, 1, LANES), F32)],
        in_specs=[VMEM],
        out_specs=[VMEM, VMEM],
        compiler_params=PARAMS,
    )(got)


def last_kernel(scale, got_ref, out_ref):
    out_ref[...] = (jnp.sum(got_ref[...], axis=0) / scale).reshape(LANES)[:R]


def last(got, scale):
    return pl.pallas_call(
        functools.partial(last_kernel, scale),
        out_shape=jax.ShapeDtypeStruct((R,), F32),
        in_specs=[VMEM],
        out_specs=VMEM,
        compiler_params=PARAMS,
    )(got)


def swaps(axes, size):
    for start in (1, 0):
        firsts = range(start, size - 1, 2)
        yield axes, [(i, i + 1) for i in firsts] + [(i + 1, i) for i in firsts]


def exchange(x, axes):
    return lax.all_to_all(x, axes, split_axis=0, concat_axis=0, tiled=True)


def shards(disp, adjoint, tiles, tile_rows, tile_cols, density, filter_weight, owner, region, face_x, face_y):
    ny, nz, nx, nc = (lax.axis_size(a) for a in ("y", "z", "x", "c"))
    scalars = [a.reshape(1, NT) for a in (density, filter_weight, owner, region)]
    ul, *faces, density, weight, owner, region = pack(face_x, face_y, disp, adjoint, *scalars)
    plans = [*swaps(("y", "z"), ny * nz), *swaps(("x", "c"), nx * nc)]
    halos = [lax.ppermute(face, axes, pairs) for face, (axes, pairs) in zip(faces, plans)]
    k, factor, wide, totals = stiffness(density, weight, owner, region, tiles)
    sent = elements(tile_rows, tile_cols, owner, region, k, factor, wide, totals, ul, *halos)
    filtered, energy = regions(exchange(sent, ("c", "x")), ny * nz)
    compliance = last(exchange(energy, ("y", "z")), math.sqrt(NT * ny * nz * nx * nc))
    return (filtered, compliance)


def solution(mesh):
    columns, rows = mesh.devices.shape
    nz = 12 if columns % 12 == 0 else columns
    parts = Mesh(mesh.devices.reshape(columns // nz, nz, rows // 2, 2), ("y", "z", "x", "c"))
    axes = ("y", "z", "x", "c")
    flat, wide, deep = P(axes), P(axes, None), P(axes, None, None)
    placed = (wide, wide, wide, flat, flat, flat, flat, wide, flat, deep, deep)
    return jax.shard_map(shards, mesh=parts, in_specs=placed, out_specs=(wide, P()), check_vma=False)
```
